32 devices in a mesh: row: 4 (over y, x), col: 8 (over z, core).
Axes of the slice: x: 2, y: 2, z: 4, core: 2. Of those that a mesh axis runs over, the one named last changes fastest.
Arguments:
- local_tiles: bfloat16 [8192, 128, 128], P(('row', 'col')), may hold values from -0.109375 to 0.109375
- local_src: int32 [8192], P(('row', 'col')), may hold values from 0 to 15
- local_dst: int32 [8192], P(('row', 'col')), may hold values from 0 to 15
- local_count: int32 [32], P(('row', 'col')), may hold values from 128 to 256, as said below
- remote_tiles: bfloat16 [2048, 128, 128], P(('row', 'col')), may hold values from -0.109375 to 0.109375
- remote_src: int32 [2048], P(('row', 'col')), may hold values from 0 to 15
- remote_dst: int32 [2048], P(('row', 'col')), may hold values from 0 to 15
- bucket_count: int32 [32, 32], P(('row', 'col')), may hold values from 1 to 2, as said below
- hub_ids: int32 [256], P(('row', 'col')), may hold values from 0 to 65535, as said below
- hub_weights: bfloat16 [256, 65536], P(None, ('row', 'col')), may hold values from -0.109375 to 0.109375
- prior: float32 [65536, 128], P(('row', 'col')), may hold values from -6 to 6
- seed_ids: int32 [128], replicated, may hold values from 0 to 65535
Outputs:
- rank_vector: float32 [65536, 128], P(('row', 'col'))
- residual: float32 [65536, 128], P(('row', 'col'))
The draws below stay inside these ranges and needn't reach their ends.
Inputs may be any that keep to these rules, and one draw needn't show every extreme that they name: `local_count`: each device has at least half of its 256 slots live; some device has all of them live. `bucket_count`: every bucket has at least one live slot; every device's bucket to some device is full, and some device receives full buckets from every device. `hub_ids`: the 8 entries of device i are distinct vertices of device i's own blocks.
All inputs are finite; a program needn't handle non-finite values.
Results may differ from the reference program's by a relative error of at most 0.009.
Values may be sent and summed in bfloat16 or wider, within the bound.
A program may use at most 128 MiB of HBM per device.

```python
import jax
import jax.numpy as jnp
from jax import lax

SEEDS = 128
BLOCK = 128
VB_DEV = 16
CAP = 2
HUB_DEV = 8
ITERS = 2
LOCAL_DEV = 256
LOCALS = 8192
SLOTS = 2048
VERTS = 65536
HUB = 256
FANIN = 2816
N_ROW = 4
N_COL = 8


def draw_local_count(key, part):
    device_count = N_ROW * N_COL
    counts = jax.random.randint(key, (device_count,), LOCAL_DEV // 2, LOCAL_DEV + 1)
    chosen = jax.random.randint(jax.random.fold_in(key, 7), (), 0, device_count)
    counts = jnp.where(jnp.arange(device_count) == chosen, LOCAL_DEV, counts)
    return counts.astype(jnp.int32)


def draw_bucket_count(key, part):
    device_count = N_ROW * N_COL
    counts = jax.random.randint(key, (device_count, device_count), 1, CAP + 1)
    chosen = jax.random.randint(jax.random.fold_in(key, 11), (), 0, device_count)
    source = jnp.arange(device_count)[:, None]
    target = jnp.arange(device_count)[None, :]
    filled = (target == chosen) | (target == (source * 7 + 3) % device_count)
    return jnp.where(filled, CAP, counts).astype(jnp.int32)


def draw_hub_ids(key, part):
    device_count = N_ROW * N_COL
    vertex_rows = VB_DEV * BLOCK
    keys = jax.random.split(key, device_count)
    picked = jax.vmap(lambda single: jax.random.permutation(single, vertex_rows)[:HUB_DEV])(keys)
    offsets = jnp.arange(device_count)[:, None] * vertex_rows
    return (picked + offsets).reshape(-1).astype(jnp.int32)


def plant(array, rng, least, top_value):
    shape = array.shape
    place = [jax.random.randint(jax.random.fold_in(rng, axis), (), 0, shape[axis]) for axis in range(len(shape))]
    array = array.at[tuple(place)].set(least)
    longest = shape.index(max(shape))
    place[longest] = (place[longest] + 1) % shape[longest]
    return array.at[tuple(place)].set(top_value)


def shard_levels(rng, extent, cuts, least, top_value):
    factor_of = 1.0
    for dim, blocks in cuts:
        heights = jax.random.uniform(jax.random.fold_in(jax.random.fold_in(rng, 6), dim), (blocks,), jnp.float32, least / len(cuts), top_value / len(cuts))
        factor_of = factor_of * jnp.repeat(jnp.exp(heights), extent[dim] // blocks).reshape((-1,) + (1,) * (len(extent) - 1 - dim))
    return factor_of


def scatter_about(own_key, shape, width, bound, pieces=(), held_as=jnp.bfloat16):
    result = width * jax.random.normal(own_key, shape, jnp.float32)
    if pieces:
        result = result * shard_levels(own_key, shape, pieces, -0.22, 0.18)
    return jnp.clip(result, -bound, bound).astype(held_as)


def setup_inputs(seed: int = 0) -> dict:
    seeds = jax.random.split(jax.random.key(seed), 13)
    local_tiles = scatter_about(seeds[0], (LOCALS, BLOCK, BLOCK), FANIN ** -0.5, 0.109375, ((0, 32),))
    local_src = plant(jax.random.randint(seeds[1], (LOCALS,), 0, VB_DEV), jax.random.fold_in(seeds[1], 1), 0, VB_DEV - 1).astype(jnp.int32)
    local_dst = plant(jax.random.randint(seeds[2], (LOCALS,), 0, VB_DEV), jax.random.fold_in(seeds[2], 1), 0, VB_DEV - 1).astype(jnp.int32)
    local_count = draw_local_count(jax.random.fold_in(seeds[12], 71), 0)
    remote_tiles = scatter_about(seeds[4], (SLOTS, BLOCK, BLOCK), FANIN ** -0.5, 0.109375, ((0, 32),))
    remote_src = plant(jax.random.randint(seeds[5], (SLOTS,), 0, VB_DEV), jax.random.fold_in(seeds[5], 1), 0, VB_DEV - 1).astype(jnp.int32)
    remote_dst = plant(jax.random.randint(seeds[6], (SLOTS,), 0, VB_DEV), jax.random.fold_in(seeds[6], 1), 0, VB_DEV - 1).astype(jnp.int32)
    bucket_count = draw_bucket_count(jax.random.fold_in(seeds[12], 71), 0)
    hub_ids = draw_hub_ids(jax.random.fold_in(seeds[12], 71), 0)
    hub_weights = scatter_about(seeds[9], (HUB, VERTS), FANIN ** -0.5, 0.109375, ((1, 32),))
    prior = scatter_about(seeds[10], (VERTS, SEEDS), 1.0, 6.0, ((0, 32),), jnp.float32)
    seed_ids = plant(jax.random.randint(seeds[11], (SEEDS,), 0, VERTS), jax.random.fold_in(seeds[11], 1), 0, VERTS - 1).astype(jnp.int32)
    return {"local_tiles": local_tiles, "local_src": local_src, "local_dst": local_dst, "local_count": local_count, "remote_tiles": remote_tiles, "remote_src": remote_src, "remote_dst": remote_dst, "bucket_count": bucket_count, "hub_ids": hub_ids, "hub_weights": hub_weights, "prior": prior, "seed_ids": seed_ids}


DAMPING = 0.85


def reference(local_tiles, local_src, local_dst, local_count, remote_tiles, remote_src, remote_dst, bucket_count, hub_ids, hub_weights, prior, seed_ids):
    device_count = N_ROW * N_COL
    vertex_rows = VB_DEV * BLOCK
    vertex_count = vertex_rows * device_count
    slot_total = device_count * CAP
    vertex_ids = jnp.arange(vertex_count, dtype=jnp.int32)
    teleport = prior + 4.0 * (vertex_ids[:, None] == seed_ids[None, :]).astype(jnp.float32)
    is_hub = jnp.zeros((vertex_count,), jnp.float32).at[hub_ids].set(1.0)
    tile_list = local_tiles.reshape(device_count, LOCAL_DEV, BLOCK, BLOCK)
    local_source = local_src.reshape(device_count, LOCAL_DEV)
    local_target = local_dst.reshape(device_count, LOCAL_DEV)
    local_live = (jnp.arange(LOCAL_DEV, dtype=jnp.int32)[None, :] < local_count[:, None]).astype(jnp.float32)
    remote_list = remote_tiles.reshape(device_count, slot_total, BLOCK, BLOCK)
    remote_source = remote_src.reshape(device_count, slot_total)
    slot_index = jnp.arange(slot_total, dtype=jnp.int32)
    remote_live = ((slot_index % CAP)[None, :] < bucket_count[:, slot_index // CAP]).astype(jnp.float32)
    block_ids = ((slot_index // CAP) * VB_DEV)[None, :] + remote_dst.reshape(device_count, slot_total)
    rank_vector = jnp.zeros((vertex_count, SEEDS), jnp.float32)
    residual = teleport
    for iteration in range(ITERS):
        sent_state = residual.astype(jnp.bfloat16)
        rank_vector = rank_vector + (1.0 - DAMPING) * residual
        masked = jnp.where(is_hub[:, None] > 0, jnp.zeros_like(sent_state), sent_state)
        own_blocks = masked.reshape(device_count, VB_DEV, BLOCK, SEEDS)

        def local_part(inputs):
            tiles_here, source, target, is_live, blocks_here = inputs
            picked = blocks_here[source].astype(jnp.float32)
            contrib = jnp.einsum('tab,tas->tbs', tiles_here.astype(jnp.float32), picked)
            select = (jnp.arange(VB_DEV, dtype=jnp.int32)[:, None] == target[None, :]).astype(jnp.float32) * is_live[None, :]
            return jnp.einsum('dt,tbs->dbs', select, contrib)

        local_terms = lax.map(local_part, (tile_list, local_source, local_target, local_live, own_blocks))

        def remote_part(running, inputs):
            tiles_here, source, is_live, targets, blocks_here = inputs
            picked = blocks_here[source].astype(jnp.float32)
            contrib = jnp.einsum('tab,tas->tbs', tiles_here.astype(jnp.float32), picked) * is_live[:, None, None]
            outgoing = lax.optimization_barrier(contrib.astype(jnp.bfloat16)).astype(jnp.float32)
            return running.at[targets].add(outgoing), None

        remote_terms, unused = lax.scan(remote_part, jnp.zeros((device_count * VB_DEV, BLOCK, SEEDS), jnp.float32), (remote_list, remote_source, remote_live, block_ids, own_blocks))
        hub_state = sent_state[hub_ids]
        hub_terms = lax.dot_general(hub_weights, hub_state, (((0,), (0,)), ((), ())), preferred_element_type=jnp.float32)
        residual = DAMPING * (local_terms.reshape(vertex_count, SEEDS) + remote_terms.reshape(vertex_count, SEEDS) + hub_terms)
    return rank_vector, residual
```

```python
import functools

import jax
import jax.numpy as jnp
from jax import lax
from jax.experimental import pallas as pl
from jax.experimental.pallas import tpu as pltpu
from jax.sharding import PartitionSpec as P

DAMPING = 0.85
AXES = ("row", "col")
VMEM = pl.BlockSpec(memory_space=pltpu.VMEM)
SMEM = pl.BlockSpec(memory_space=pltpu.SMEM)
TAIL = 16
LIMIT = 56 * 1024 * 1024


def teleport_block(prior, seeds, block, tile):
    rows = lax.broadcasted_iota(jnp.int32, (tile, prior.shape[1]), 0) + block * tile
    return prior[pl.ds(block * tile, tile), :] + jnp.where(rows == seeds[...], 4.0, 0.0)


def push(src, dst, live, hubs, tiles, work, hub_rows, state, out):
    slots, tile, _ = tiles.shape
    blocks = state.shape[0]
    devices = live.shape[1]
    cap = slots // devices
    hub_dev = hubs.shape[0]
    for h in range(hub_dev):
        hub_rows[pl.ds(h, 1), :] = work[pl.ds(hubs[h], 1), :]
    for h in range(hub_dev):
        work[pl.ds(hubs[h], 1), :] = jnp.zeros((1, work.shape[1]), jnp.float32)

    def turn(block, carry):
        state[block] = work[pl.ds(block * tile, tile), :].T.astype(jnp.bfloat16)
        return carry

    lax.fori_loop(0, blocks, turn, 0, unroll=4)

    def send(k, carry):
        tail = hub_rows[...]
        rows = lax.broadcasted_iota(jnp.int32, tail.shape, 0)
        for c in range(cap):
            tail = jnp.where(rows == hub_dev + c, dst[k * cap + c].astype(jnp.float32), tail)
        out[k, cap * tile :, :] = tail.astype(jnp.bfloat16)
        for c in range(cap):
            j = k * cap + c
            value = jnp.dot(state[src[j]], tiles[j], preferred_element_type=jnp.float32)
            value = jnp.where(live[0, k] > c, value, 0.0)
            out[k, c * tile : (c + 1) * tile, :] = value.astype(jnp.bfloat16)
        return carry

    lax.fori_loop(0, devices, send, 0, unroll=4)


def first_kernel(src, dst, live, hubs, seeds, prior, tiles, out, state, work, hub_rows):
    tile = tiles.shape[1]

    def begin(block, carry):
        work[pl.ds(block * tile, tile), :] = teleport_block(prior, seeds, block, tile)
        return carry

    lax.fori_loop(0, state.shape[0], begin, 0, unroll=4)
    hub_rows[...] = jnp.zeros_like(hub_rows)
    push(src, dst, live, hubs, tiles, work, hub_rows, state, out)


def local_kernel(src, dst, count, tiles, state, total):
    step = pl.program_id(0)
    chunk = tiles.shape[0]
    unroll = 8

    @pl.when(step == 0)
    def _():
        total[...] = jnp.zeros_like(total)

    first = step * chunk
    here = jnp.clip(count[0] - first, 0, chunk)

    def several(i, carry):
        values = []
        for u in range(unroll):
            t = i * unroll + u
            values.append(
                jnp.dot(state[src[first + t]], tiles[t], preferred_element_type=jnp.float32)
            )
        for u in range(unroll):
            t = i * unroll + u
            total[dst[first + t]] += jnp.where(t < here, values[u], 0.0)
        return carry

    lax.fori_loop(0, (here + unroll - 1) // unroll, several, 0)


def gather_terms(incoming, targets, total, acc):
    devices = incoming.shape[0]
    tile = total.shape[1]
    cap = targets.shape[0] // devices
    acc[...] = total[...]

    def add(k, carry):
        for c in range(cap):
            part = incoming[k, c * tile : (c + 1) * tile, :].astype(jnp.float32)
            acc[targets[k * cap + c]] += part
        return carry

    lax.fori_loop(0, devices, add, 0, unroll=2)


def hub_states(incoming, hub_all, hub_dev, cap, ints=None):
    devices, rows, _ = incoming.shape

    def take(k, carry):
        tail = incoming[k, rows - TAIL :, :].astype(jnp.float32)
        hub_all[pl.ds(k * hub_dev, hub_dev), :] = tail[:hub_dev]
        if ints is not None:
            ints[pl.ds(k * 8, 8), :] = tail[hub_dev : hub_dev + 8].astype(jnp.int32)
        return carry

    lax.fori_loop(0, devices, take, 0, unroll=4)
    return hub_all[...].T.astype(jnp.bfloat16)


def middle_kernel(
    src, dst, live, hubs, seeds, prior, tiles, incoming, total, weights,
    out, state, rank, targets, work, hub_rows, acc, hub_all, ints, ints_smem, sem,
):
    tile = tiles.shape[1]
    blocks = state.shape[0]
    devices = live.shape[1]
    cap = tiles.shape[0] // devices
    hub_dev = hubs.shape[0]
    hub_state = hub_states(incoming, hub_all, hub_dev, cap, ints)
    copy = pltpu.make_async_copy(ints, ints_smem, sem)
    copy.start()
    copy.wait()
    for c in range(cap):

        def fill(k, carry, c=c):
            targets[k * cap + c] = ints_smem[k * 8 + c, 0]
            return carry

        lax.fori_loop(0, devices, fill, 0, unroll=8)
    gather_terms(incoming, targets, total, acc)
    for block in range(blocks):
        rows = pl.ds(block * tile, tile)
        hub = jnp.dot(hub_state, weights[:, rows], preferred_element_type=jnp.float32)
        residual = (DAMPING * (acc[block] + hub)).T
        work[rows, :] = residual
        rank[rows, :] = (1.0 - DAMPING) * teleport_block(prior, seeds, block, tile) + (
            1.0 - DAMPING
        ) * residual
    hub_rows[...] = jnp.zeros_like(hub_rows)
    push(src, dst, live, hubs, tiles, work, hub_rows, state, out)


def last_kernel(hub_dev, targets, incoming, total, weights, residual, acc, hub_all):
    blocks, tile, _ = total.shape
    cap = targets.shape[0] // incoming.shape[0]
    hub_state = hub_states(incoming, hub_all, hub_dev, cap)
    gather_terms(incoming, targets, total, acc)
    for block in range(blocks):
        rows = pl.ds(block * tile, tile)
        hub = jnp.dot(hub_state, weights[:, rows], preferred_element_type=jnp.float32)
        residual[rows, :] = (DAMPING * (acc[block] + hub)).T


def body(
    local_tiles, local_src, local_dst, local_count, remote_tiles, remote_src,
    remote_dst, bucket_count, hub_ids, hub_weights, prior, seed_ids,
):
    devices = lax.axis_size(AXES)
    own = lax.axis_index(AXES)
    vertex_rows, seeds = prior.shape
    tile = local_tiles.shape[1]
    blocks = vertex_rows // tile
    slots = remote_src.shape[0]
    cap = slots // devices
    hub_dev = hub_ids.shape[0]
    local_slots = local_src.shape[0]
    rows = cap * tile + TAIL
    hubs = hub_ids - own * vertex_rows
    seed_rows = (seed_ids - own * vertex_rows).reshape(1, seeds)

    f32, bf16, i32 = jnp.float32, jnp.bfloat16, jnp.int32
    payload = jax.ShapeDtypeStruct((devices, rows, seeds), bf16)
    state_shape = jax.ShapeDtypeStruct((blocks, seeds, tile), bf16)
    total_shape = jax.ShapeDtypeStruct((blocks, seeds, tile), f32)
    vertex_shape = jax.ShapeDtypeStruct((vertex_rows, seeds), f32)
    work = pltpu.VMEM((vertex_rows, seeds), f32)
    hub_rows = pltpu.VMEM((TAIL, seeds), f32)
    acc = pltpu.VMEM((blocks, seeds, tile), f32)
    hub_all = pltpu.VMEM((devices * hub_dev, seeds), f32)
    params = pltpu.CompilerParams(vmem_limit_bytes=LIMIT)

    out, state = pl.pallas_call(
        first_kernel,
        out_shape=(payload, state_shape),
        in_specs=[SMEM] * 4 + [VMEM] * 3,
        out_specs=(VMEM, VMEM),
        scratch_shapes=[work, hub_rows],
        compiler_params=params,
    )(remote_src, remote_dst, bucket_count, hubs, seed_rows, prior, remote_tiles)

    def exchange(array):
        return lax.all_to_all(array, AXES, split_axis=0, concat_axis=0, tiled=True)

    chunk = 32

    def local(state):
        return pl.pallas_call(
            local_kernel,
            grid=(local_slots // chunk,),
            out_shape=total_shape,
            in_specs=[SMEM, SMEM, SMEM]
            + [
                pl.BlockSpec((chunk, tile, tile), lambda i: (i, 0, 0)),
                pl.BlockSpec((blocks, seeds, tile), lambda i: (0, 0, 0)),
            ],
            out_specs=pl.BlockSpec((blocks, seeds, tile), lambda i: (0, 0, 0)),
            compiler_params=params,
            cost_estimate=pl.CostEstimate(
                flops=2 * local_slots * tile * tile * seeds,
                bytes_accessed=local_slots * tile * tile * 2,
                transcendentals=0,
            ),
        )(local_src, local_dst, local_count, local_tiles, state)

    incoming = exchange(out)
    total = local(state)
    out, state, rank, targets = pl.pallas_call(
        middle_kernel,
        out_shape=(payload, state_shape, vertex_shape, jax.ShapeDtypeStruct((slots,), i32)),
        in_specs=[SMEM] * 4 + [VMEM] * 6,
        out_specs=(VMEM, VMEM, VMEM, SMEM),
        scratch_shapes=[
            work, hub_rows, acc, hub_all,
            pltpu.VMEM((devices * 8, seeds), i32),
            pltpu.SMEM((devices * 8, seeds), i32),
            pltpu.SemaphoreType.DMA,
        ],
        compiler_params=params,
    )(
        remote_src, remote_dst, bucket_count, hubs, seed_rows, prior, remote_tiles,
        incoming, total, hub_weights,
    )
    incoming = exchange(out)
    total = local(state)
    residual = pl.pallas_call(
        functools.partial(last_kernel, hub_dev),
        out_shape=vertex_shape,
        in_specs=[SMEM] + [VMEM] * 3,
        out_specs=VMEM,
        scratch_shapes=[acc, hub_all],
        compiler_params=params,
    )(targets, incoming, total, hub_weights)
    return rank, residual


def solution(mesh):
    both = P(AXES)
    placed = (
        P(AXES, None, None), both, both, both, P(AXES, None, None), both,
        both, P(AXES, None), both, P(None, AXES), P(AXES, None), P(),
    )
    return jax.shard_map(
        body,
        mesh=mesh,
        in_specs=placed,
        out_specs=(P(AXES, None), P(AXES, None)),
        check_vma=False,
    )
```

```python
import functools

import jax
import jax.numpy as jnp
from jax import lax
from jax.experimental import pallas as pl
from jax.experimental.pallas import tpu as pltpu
from jax.sharding import PartitionSpec as P

DAMPING = 0.85
ITERS = 2
AXES = ("row", "col")
VMEM = pl.BlockSpec(memory_space=pltpu.VMEM)
SMEM = pl.BlockSpec(memory_space=pltpu.SMEM)
ANY = pl.BlockSpec(memory_space=pl.ANY)
TAIL = 16
LIMIT = 62 * 1024 * 1024
MESH = pl.DeviceIdType.MESH
f32, bf16, i32 = jnp.float32, jnp.bfloat16, jnp.int32


def iota(shape, axis):
    return lax.broadcasted_iota(i32, shape, axis)


def sort_tables(keys, blocks):
    n = keys.shape[0]
    index = jnp.arange(n, dtype=i32)
    row, column = keys[None, :], keys[:, None]
    before = (row < column) | ((row == column) & (index[None, :] < index[:, None]))
    place = jnp.sum(before.astype(i32), axis=1)
    hit = place[:, None] == index[None, :]
    order = jnp.sum(jnp.where(hit, index[:, None], 0), axis=0)
    starts = jnp.sum((column < jnp.arange(blocks + 1, dtype=i32)[None, :]).astype(i32), axis=0)
    return order, starts


def kernel(
    n_col, cap, src, live, hubs, lsrc, lorder, lstart, rdev, rslot, rstart, seeds, prior,
    weights, tiles, ltiles,
    rank, res, out, recv_first, recv_last, state, lt, sums, total, hub_rows, hub_all,
    send_sem, recv_sem, tile_sem,
):
    recvs = (recv_first, recv_last)
    devices = live.shape[1]
    slots, tile, _ = tiles.shape
    vertex_rows, columns = prior.shape
    blocks = vertex_rows // tile
    half = columns // 2
    hub_dev = hubs.shape[0]
    local_slots = lt.shape[0]
    me = lax.axis_index("row") * n_col + lax.axis_index("col")
    base = me * vertex_rows

    fetch = pltpu.make_async_copy(ltiles, lt, tile_sem)
    fetch.start()

    def device(k):
        return (k // n_col, k % n_col)

    barrier = pltpu.get_barrier_semaphore()

    def greet(o, carry):
        k = lax.rem(me + o, devices)
        pl.semaphore_signal(barrier, inc=1, device_id=device(k), device_id_type=MESH)
        return carry

    lax.fori_loop(1, devices, greet, 0)

    def teleport(block):
        rows = iota((tile, columns), 0) + (base + block * tile)
        return prior[pl.ds(block * tile, tile), :] + jnp.where(rows == seeds[...], 4.0, 0.0)

    def begin(block, carry):
        res[pl.ds(block * tile, tile), :] = teleport(block)
        return carry

    lax.fori_loop(0, blocks, begin, 0, unroll=4)
    hub_rows[...] = jnp.zeros_like(hub_rows)

    def partner_copy(r, o):
        k = lax.rem(me + o, devices)
        return pltpu.make_async_remote_copy(
            src_ref=out.at[k],
            dst_ref=recvs[r].at[me],
            send_sem=send_sem.at[r, o],
            recv_sem=recv_sem.at[r, o],
            device_id=device(k),
            device_id_type=MESH,
        )

    for r in range(ITERS):
        def turn(block, found):
            rows = iota((tile, columns), 0) + (base + block * tile)
            value = res[pl.ds(block * tile, tile), :]
            is_hub = rows == hubs[0]
            for h in range(1, hub_dev):
                is_hub = is_hub | (rows == hubs[h])
            state[block] = jnp.where(is_hub, 0.0, value).T.astype(bf16)
            more = []
            for h in range(hub_dev):
                part = jnp.where(rows == hubs[h], value, 0.0).reshape(tile // 8, 8, columns)
                more.append(found[h] + jnp.sum(part, axis=0))
            return tuple(more)

        nothing = tuple(jnp.zeros((8, columns), f32) for h in range(hub_dev))
        found = lax.fori_loop(0, blocks, turn, nothing)
        for h in range(hub_dev):
            hub_rows[h : h + 1, :] = jnp.sum(found[h], axis=0, keepdims=True)

        def payload(k, store):
            store(cap * tile, TAIL, hub_rows[...].astype(bf16))
            for c in range(cap):
                j = k * cap + c
                value = jnp.dot(state[src[j]], tiles[j], preferred_element_type=f32)
                value = value * (live[0, k] > c).astype(f32)
                store(c * tile, tile, value.astype(bf16))

        if r == 0:
            pl.semaphore_wait(barrier, devices - 1)

        def send(o, carry, r=r):
            k = lax.rem(me + o, devices)

            def store(at, size, value):
                out[k, at : at + size, :] = value

            payload(k, store)
            partner_copy(r, o).start()
            return carry

        lax.fori_loop(1, devices, send, 0)

        def keep(at, size, value, r=r):
            recvs[r][me, at : at + size, :] = value

        payload(me, keep)

        if r == 0:
            fetch.wait()

        def finish(start, h, add):
            for d in range(blocks):
                value = sums[start[d + 1]] - sums[start[d]]
                where = slice(h * half, (h + 1) * half)
                if add:
                    total[d, where, :] += value
                else:
                    total[d, where, :] = value

        sums[0] = jnp.zeros((half, tile), f32)
        for h in range(2):

            def local(t, acc, h=h):
                p = lorder[t]
                left = state[lsrc[p], h * half : (h + 1) * half, :]
                acc = acc + jnp.dot(left, lt[p], preferred_element_type=f32)
                sums[t + 1] = acc
                return acc

            lax.fori_loop(0, local_slots, local, jnp.zeros((half, tile), f32), unroll=8)
            finish(lstart, h, False)

        def arrive(o, carry, r=r):
            partner_copy(r, o).wait()
            return carry

        lax.fori_loop(1, devices, arrive, 0)

        def take(k, carry, r=r):
            tail = recvs[r][k, cap * tile :, :].astype(f32)
            hub_all[pl.ds(k * hub_dev, hub_dev), :] = tail[:hub_dev]
            return carry

        lax.fori_loop(0, devices, take, 0, unroll=4)
        for h in range(2):

            def remote(t, acc, h=h, r=r):
                part = 0.0
                for c in range(cap):
                    at = c * tile + h * half
                    here = recvs[r][rdev[t], at : at + half, :].astype(f32)
                    part = part + here * (rslot[t] == c).astype(f32)
                acc = acc + part
                sums[t + 1] = acc
                return acc

            lax.fori_loop(0, slots, remote, jnp.zeros((half, tile), f32), unroll=8)
            finish(rstart, h, True)

        hub_state = hub_all[...].T.astype(bf16)

        def combine(block, carry, r=r, hub_state=hub_state):
            rows = pl.ds(pl.multiple_of(block * tile, tile), tile)
            hub = jnp.dot(hub_state, weights[:, rows], preferred_element_type=f32)
            residual = (DAMPING * (total[block] + hub)).T
            if r == 0:
                rank[rows, :] = (1.0 - DAMPING) * teleport(block) + (1.0 - DAMPING) * residual
            res[rows, :] = residual
            return carry

        lax.fori_loop(0, blocks, combine, 0, unroll=2)


def body(
    n_col, local_tiles, local_src, local_dst, local_count, remote_tiles, remote_src,
    remote_dst, bucket_count, hub_ids, hub_weights, prior, seed_ids,
):
    devices = lax.axis_size(AXES)
    vertex_rows, columns = prior.shape
    tile = local_tiles.shape[1]
    blocks = vertex_rows // tile
    slots = remote_src.shape[0]
    cap = slots // devices
    hub_dev = hub_ids.shape[0]
    local_slots = local_src.shape[0]
    rows = cap * tile + TAIL
    vertex = jax.ShapeDtypeStruct((vertex_rows, columns), f32)
    targets = lax.all_to_all(
        remote_dst.reshape(devices, cap), AXES, split_axis=0, concat_axis=0, tiled=True
    ).reshape(-1)
    living = jnp.arange(local_slots, dtype=i32) < local_count[0]
    lorder, lstart = sort_tables(jnp.where(living, local_dst, blocks), blocks)
    rorder, rstart = sort_tables(targets, blocks)
    return pl.pallas_call(
        functools.partial(kernel, n_col, cap),
        out_shape=(vertex, vertex),
        in_specs=[SMEM] * 9 + [VMEM] * 4 + [ANY],
        out_specs=(VMEM, VMEM),
        scratch_shapes=[
            pltpu.VMEM((devices, rows, columns), bf16),
            pltpu.VMEM((devices, rows, columns), bf16),
            pltpu.VMEM((devices, rows, columns), bf16),
            pltpu.VMEM((blocks, columns, tile), bf16),
            pltpu.VMEM(local_tiles.shape, bf16),
            pltpu.VMEM((max(local_slots, slots) + 1, columns // 2, tile), f32),
            pltpu.VMEM((blocks, columns, tile), f32),
            pltpu.VMEM((TAIL, columns), f32),
            pltpu.VMEM((devices * hub_dev, columns), f32),
            pltpu.SemaphoreType.DMA((ITERS, devices)),
            pltpu.SemaphoreType.DMA((ITERS, devices)),
            pltpu.SemaphoreType.DMA,
        ],
        compiler_params=pltpu.CompilerParams(
            collective_id=0, has_side_effects=True, vmem_limit_bytes=LIMIT
        ),
    )(
        remote_src, bucket_count, hub_ids, local_src, lorder, lstart, rorder // cap, rorder % cap,
        rstart, seed_ids.reshape(1, columns), prior,
        hub_weights, remote_tiles, local_tiles,
    )


def solution(mesh):
    both = P(AXES)
    placed = (
        P(AXES, None, None), both, both, both, P(AXES, None, None), both,
        both, P(AXES, None), both, P(None, AXES), P(AXES, None), P(),
    )
    return jax.shard_map(
        functools.partial(body, mesh.shape["col"]),
        mesh=mesh,
        in_specs=placed,
        out_specs=(P(AXES, None), P(AXES, None)),
        check_vma=False,
    )
```
